512 devices in a mesh: site: 16 (over z), bond: 32 (over y, x, core).
Axes of the slice: x: 4, y: 4, z: 16, core: 2. Of those that a mesh axis runs over, the one named last changes fastest.
Arguments:
- site_tensor: float32 [16, 4, 3072, 3072], P('site', None, 'bond'), may hold values from -0.21875 to 0.21875
- panels: float32 [16, 3072, 128], P('site', 'bond'), may hold values from -6 to 6
- fresh: float32 [1, 3072, 128], P(None, 'bond'), may hold values from -6 to 6
- outcomes: int32 [16, 2, 128], P('site'), may hold values from 0 to 3, as said below
Outputs:
- carried: float32 [16, 2, 3072, 128], P('site', None, 'bond')
The draws below stay inside these ranges and needn't reach their ends.
Inputs may be any that keep to these rules, and one draw needn't show every extreme that they name: `outcomes`: at each site and tick, every outcome is taken by at most 48 samples, and some outcome by exactly 48.
All inputs are finite; a program needn't handle non-finite values.
Results may differ from the reference program's by a relative error of at most 0.0001.
Values sent between devices are 32-bit elements; how exact they have to be, the bound alone decides.
No kernel may reach another device: no remote copies, remote signals or barrier semaphores. Data moves between devices by JAX's collectives and lax.ppermute only.
A program may use at most 64 MiB of HBM per device.

```python
import jax
import jax.numpy as jnp
from jax import lax

CHI = 3072
OUTCOMES = 4
SAMPLES = 128
TICKS = 2
SITES = 16


def draw_outcomes(key, part):
    site_keys = jax.random.split(jax.random.fold_in(key, 7), SITES * TICKS)

    def draw_single(one_key):
        key_first, key_second, key_order, key_shuffle = jax.random.split(one_key, 4)
        most_count = SAMPLES * 3 // 8
        remaining = SAMPLES - most_count
        count_first = jax.random.randint(key_first, (), 0, most_count + 1)
        lower_bound = jnp.maximum(0, remaining - count_first - most_count)
        upper_bound = jnp.minimum(most_count, remaining - count_first)
        count_second = jax.random.randint(key_second, (), lower_bound, upper_bound + 1)
        count_third = remaining - count_first - count_second
        counts_all = jnp.stack([jnp.int32(most_count), count_first.astype(jnp.int32), count_second.astype(jnp.int32), count_third.astype(jnp.int32)])
        outcome_order = jax.random.permutation(key_order, 4).astype(jnp.int32)
        boundaries = jnp.cumsum(counts_all)
        position = jnp.arange(SAMPLES, dtype=jnp.int32)
        bucket_slot = jnp.sum((position[:, None] >= boundaries[None, :]).astype(jnp.int32), axis=1)
        labelled = outcome_order[bucket_slot]
        return jax.random.permutation(key_shuffle, labelled).astype(jnp.int32)
    return jax.vmap(draw_single)(site_keys).reshape(SITES, TICKS, SAMPLES)


def strengthened(drawn, key, source, target, shards_of, factor):
    def block_of(axis_at):
        return (jnp.arange(drawn.shape[axis_at]) // (drawn.shape[axis_at] // shards_of)).reshape((-1,) + (1,) * (drawn.ndim - 1 - axis_at))

    near = jax.random.permutation(key, shards_of)[block_of(target)]
    far = (block_of(target) + shards_of // 2) % shards_of
    return jnp.where((block_of(source) == near) | (block_of(source) == far), factor * drawn, drawn)


def shard_levels(own_key, dims, pieces, low, high):
    gain = 1.0
    for axis_at, parts in pieces:
        draws = jax.random.uniform(jax.random.fold_in(jax.random.fold_in(own_key, 6), axis_at), (parts,), jnp.float32, low / len(pieces), high / len(pieces))
        gain = gain * jnp.repeat(jnp.exp(draws), dims[axis_at] // parts).reshape((-1,) + (1,) * (len(dims) - 1 - axis_at))
    return gain


def scatter_about(stream_key, extent, scale, reach, shards=(), kind=jnp.bfloat16):
    entries = scale * jax.random.normal(stream_key, extent, jnp.float32)
    if shards:
        entries = entries * shard_levels(stream_key, extent, shards, -0.22, 0.18)
    return jnp.clip(entries, -reach, reach).astype(kind)


def noise_with(own_key, dims, width, limit, cuts, heavy, kind=jnp.bfloat16):
    array = width * jax.random.normal(own_key, dims, jnp.float32)
    if cuts:
        array = array * shard_levels(own_key, dims, cuts, -0.22, 0.18)
    return jnp.clip(strengthened(array, jax.random.fold_in(own_key, 3), *heavy), -limit, limit).astype(kind)


def setup_inputs(seed: int = 0) -> dict:
    splits = jax.random.split(jax.random.key(seed), 5)
    return {
        "site_tensor": noise_with(splits[0], (SITES, OUTCOMES, CHI, CHI), CHI ** -0.5, 0.21875, ((0, 16), (2, 32)), (2, 3, 32, 2.75), jnp.float32),
        "panels": scatter_about(splits[1], (SITES, CHI, SAMPLES), 1.0, 6.0, ((0, 16), (1, 32)), jnp.float32),
        "fresh": scatter_about(splits[2], (TICKS - 1, CHI, SAMPLES), 1.0, 6.0, ((1, 32),), jnp.float32),
        "outcomes": draw_outcomes(jax.random.fold_in(splits[4], 71), 0),
    }


def advance(tensor, vectors, selected):
    accumulated = jnp.zeros((tensor.shape[2], vectors.shape[1]), jnp.float32)
    for outcome_index in range(tensor.shape[0]):
        column_mask = (selected == outcome_index).astype(jnp.float32)
        masked = vectors * column_mask[None, :]
        accumulated = accumulated + jnp.dot(tensor[outcome_index].T, masked, precision=lax.Precision.HIGHEST, preferred_element_type=jnp.float32)
    return accumulated


def reference(site_tensor, panels, fresh, outcomes):
    current = panels
    results = []
    for tick_index in range(TICKS):
        produced = []
        for site_index in range(SITES):
            produced.append(advance(site_tensor[site_index], current[site_index], outcomes[site_index, tick_index]))
        stacked = jnp.stack(produced, 0)
        results.append(stacked)
        if tick_index + 1 < TICKS:
            current = jnp.concatenate([fresh[tick_index][None], stacked[:-1]], 0)
    return jnp.stack(results, 1)
```

```python
import jax
import jax.numpy as jnp
from jax import lax
from jax.sharding import Mesh, PartitionSpec as P

TICKS = 2
CHIPS = ("y", "x")
BOND = ("y", "x", "core")


def contribute(tensor, vectors, selected):
    outcome_count, rows, columns = tensor.shape
    chosen = selected[None, :] == jnp.arange(outcome_count, dtype=jnp.int32)[:, None]
    masked = jnp.where(chosen[:, None, :], vectors[None], 0.0)
    return lax.dot_general(
        tensor.reshape(outcome_count * rows, columns),
        masked.reshape(outcome_count * rows, -1),
        (((0,), (0,)), ((), ())),
        precision=lax.Precision.HIGH,
        preferred_element_type=jnp.float32,
    )


def scatter_sum(partial, rows, chips):
    core = lax.axis_index("core")
    blocks = partial.reshape(chips, 2, rows, partial.shape[-1])
    kept = lax.dynamic_index_in_dim(blocks, core, 1, keepdims=False)
    sent = lax.dynamic_index_in_dim(blocks, 1 - core, 1, keepdims=False)
    paired = kept + lax.ppermute(sent, "core", [(0, 1), (1, 0)])
    return lax.all_to_all(paired, CHIPS, 0, 0, tiled=True).sum(0)


def on_device(site_tensor, panels, fresh, outcomes):
    tensor = site_tensor[0]
    rows = tensor.shape[1]
    chips = tensor.shape[2] // rows // 2
    sites = lax.axis_size("site")
    current = panels[0]
    results = []
    for tick in range(TICKS):
        partial = contribute(tensor, current, outcomes[0, tick])
        produced = scatter_sum(partial, rows, chips)
        results.append(produced)
        if tick + 1 < TICKS:
            passed = lax.ppermute(produced, "site", [(i, i + 1) for i in range(sites - 1)])
            current = jnp.where(lax.axis_index("site") == 0, fresh[tick], passed)
    return jnp.stack(results, 0)[None]


def solution(mesh):
    sites, bonds = mesh.devices.shape
    side = round((bonds // 2) ** 0.5)
    split = Mesh(mesh.devices.reshape(sites, side, side, 2), ("site", "y", "x", "core"))
    placed = (
        P("site", None, BOND, None),
        P("site", BOND, None),
        P(None, BOND, None),
        P("site", None, None),
    )
    return jax.shard_map(
        on_device,
        mesh=split,
        in_specs=placed,
        out_specs=P("site", None, BOND, None),
        check_vma=False,
    )
```

```python
import functools

import jax
import jax.numpy as jnp
from jax import lax
from jax.experimental import pallas as pl
from jax.experimental.pallas import tpu as pltpu
from jax.sharding import Mesh, PartitionSpec as P

TICKS = 2
CHIPS = ("y", "x")
BOND = ("y", "x", "core")
PARAMS = pltpu.CompilerParams(vmem_limit_bytes=24 * 1024 * 1024)
VMEM = pl.BlockSpec(memory_space=pltpu.VMEM)
HBM = pl.BlockSpec(memory_space=pltpu.HBM)


def halves(value):
    upper = value.astype(jnp.bfloat16)
    return upper, (value - upper.astype(jnp.float32)).astype(jnp.bfloat16)


def left_operand(vectors, selected, outcome_count):
    masked = [jnp.where(selected == outcome, vectors, 0.0) for outcome in range(outcome_count)]
    upper, rest = halves(jnp.concatenate(masked, axis=0).T)
    return jnp.concatenate([upper, upper, rest], axis=1)


def place_product(left, upper, rest, first, rows, core, kept_ref, sent_ref):
    right = jnp.concatenate([upper, rest, upper], axis=0)
    product = jnp.dot(left, right, preferred_element_type=jnp.float32)
    chips = product.shape[1] // (2 * rows)
    blocks = product.T.reshape(chips, 2, rows, product.shape[0])
    kept_ref[first : first + chips] = jnp.where(core == 0, blocks[:, 0], blocks[:, 1])
    sent_ref[first : first + chips] = jnp.where(core == 0, blocks[:, 1], blocks[:, 0])


def first_kernel(
    selected_hbm, vectors_hbm, tensor_hbm,
    kept_ref, sent_ref, halves_ref, selected_ref,
    vectors_ref, tensor_ref, small_sem, tensor_sem,
):
    _, outcome_count, rows, columns = tensor_hbm.shape
    pieces = 2
    width = columns // pieces
    small = [
        pltpu.make_async_copy(selected_hbm, selected_ref, small_sem.at[0]),
        pltpu.make_async_copy(vectors_hbm, vectors_ref, small_sem.at[1]),
    ]
    large = []
    for piece in range(pieces):
        columns_of = pl.ds(piece * width, width)
        large.append(
            pltpu.make_async_copy(
                tensor_hbm.at[0, :, :, columns_of],
                tensor_ref.at[:, :, columns_of],
                tensor_sem.at[piece],
            )
        )
    for copy in small + large:
        copy.start()
    for copy in small:
        copy.wait()
    left = left_operand(vectors_ref[0], selected_ref[0, 0:1], outcome_count)
    for piece in range(pieces):
        large[piece].wait()
        span = slice(piece * width, (piece + 1) * width)
        upper, rest = halves(tensor_ref[:, :, span].reshape(outcome_count * rows, width))
        halves_ref[: outcome_count * rows, span] = upper
        halves_ref[outcome_count * rows :, span] = rest
        first = piece * width // (2 * rows)
        place_product(left, upper, rest, first, rows, lax.axis_index("core"), kept_ref, sent_ref)


def later_kernel(tick, selected_ref, fresh_ref, passed_ref, halves_ref, kept_ref, sent_ref):
    rows = passed_ref.shape[0]
    vectors = jnp.where(lax.axis_index("site") == 0, fresh_ref[tick - 1], passed_ref[...])
    stacked, columns = halves_ref.shape[0] // 2, halves_ref.shape[1]
    left = left_operand(vectors, selected_ref[0, tick : tick + 1], stacked // rows)
    pieces = 2
    width = columns // pieces
    for piece in range(pieces):
        span = slice(piece * width, (piece + 1) * width)
        first = piece * width // (2 * rows)
        upper, rest = halves_ref[:stacked, span], halves_ref[stacked:, span]
        place_product(left, upper, rest, first, rows, lax.axis_index("core"), kept_ref, sent_ref)


def cost(stacked, columns, samples, read):
    return pl.CostEstimate(
        flops=6 * stacked * columns * samples, bytes_accessed=read, transcendentals=0
    )


def first_product(outcomes, panels, site_tensor):
    _, outcome_count, rows, columns = site_tensor.shape
    samples = panels.shape[-1]
    stacked = outcome_count * rows
    block = pltpu.VMEM((columns // (2 * rows), rows, samples), jnp.float32)
    both = pltpu.VMEM((2 * stacked, columns), jnp.bfloat16)
    in_hbm = [pltpu.with_memory_space_constraint(a, pltpu.HBM) for a in (outcomes, panels, site_tensor)]
    return pl.pallas_call(
        first_kernel,
        out_shape=[block, block, both, pltpu.VMEM(outcomes.shape, outcomes.dtype)],
        in_specs=[HBM, HBM, HBM],
        out_specs=[VMEM] * 4,
        scratch_shapes=[
            pltpu.VMEM(panels.shape, panels.dtype),
            pltpu.VMEM((outcome_count, rows, columns), jnp.float32),
            pltpu.SemaphoreType.DMA((2,)),
            pltpu.SemaphoreType.DMA((2,)),
        ],
        compiler_params=PARAMS,
        cost_estimate=cost(stacked, columns, samples, 4 * stacked * columns),
        name="first_product",
    )(*in_hbm)


def later_product(tick, selected, fresh, passed, both):
    rows, samples = passed.shape
    stacked, columns = both.shape[0] // 2, both.shape[1]
    block = pltpu.VMEM((columns // (2 * rows), rows, samples), jnp.float32)
    return pl.pallas_call(
        functools.partial(later_kernel, tick),
        out_shape=[block, block],
        in_specs=[VMEM, VMEM, VMEM, VMEM],
        out_specs=[VMEM] * 2,
        compiler_params=PARAMS,
        cost_estimate=cost(stacked, columns, samples, 4 * columns * samples),
        name="later_product",
    )(selected, fresh, passed, both)


def scatter_sum(kept, sent):
    paired = kept + lax.ppermute(sent, "core", [(0, 1), (1, 0)])
    arrived = lax.all_to_all(paired, CHIPS, 0, 0, tiled=True)
    total = functools.reduce(jnp.add, [arrived[chip] for chip in range(arrived.shape[0])])
    return lax.optimization_barrier(total)


def on_device(site_tensor, panels, fresh, outcomes):
    sites = lax.axis_size("site")
    kept, sent, both, selected = first_product(outcomes, panels, site_tensor)
    results = [scatter_sum(kept, sent)]
    for tick in range(1, TICKS):
        passed = lax.ppermute(results[-1], "site", [(i, i + 1) for i in range(sites - 1)])
        results.append(scatter_sum(*later_product(tick, selected, fresh, passed, both)))
    return jnp.stack(results, 0)[None]


def solution(mesh):
    sites, bonds = mesh.devices.shape
    side = round((bonds // 2) ** 0.5)
    split = Mesh(mesh.devices.reshape(sites, side, side, 2), ("site", "y", "x", "core"))
    placed = (
        P("site", None, BOND, None),
        P("site", BOND, None),
        P(None, BOND, None),
        P("site", None, None),
    )
    return jax.shard_map(
        on_device,
        mesh=split,
        in_specs=placed,
        out_specs=P("site", None, BOND, None),
        check_vma=False,
    )
```

```python
import functools

import jax
import jax.numpy as jnp
from jax import lax
from jax.experimental import pallas as pl
from jax.experimental.pallas import tpu as pltpu
from jax.sharding import Mesh, PartitionSpec as P

TICKS = 2
CHIPS = ("y", "x")
BOND = ("y", "x", "core")
PARAMS = pltpu.CompilerParams(vmem_limit_bytes=24 * 1024 * 1024)
VMEM = pl.BlockSpec(memory_space=pltpu.VMEM)
HBM = pl.BlockSpec(memory_space=pltpu.HBM)


def halves(value):
    upper = value.astype(jnp.bfloat16)
    return upper, (value - upper.astype(jnp.float32)).astype(jnp.bfloat16)


def left_operand(vectors, selected, outcome_count):
    masked = [jnp.where(selected == outcome, vectors, 0.0) for outcome in range(outcome_count)]
    upper, rest = halves(jnp.concatenate(masked, axis=0).T)
    return jnp.concatenate([upper, upper, rest], axis=1)


def place_product(left, upper, rest, first, rows, core, kept_ref, sent_ref):
    right = jnp.concatenate([upper, rest, upper], axis=0)
    product = jnp.dot(left, right, preferred_element_type=jnp.float32)
    chips = product.shape[1] // (2 * rows)
    blocks = product.T.reshape(chips, 2, rows, product.shape[0])
    kept_ref[first : first + chips] = jnp.where(core == 0, blocks[:, 0], blocks[:, 1])
    sent_ref[first : first + chips] = jnp.where(core == 0, blocks[:, 1], blocks[:, 0])


def first_kernel(
    selected_hbm, vectors_hbm, fresh_hbm, tensor_hbm,
    kept_ref, sent_ref, tensor_ref, selected_ref,
    vectors_ref, small_sem, tensor_sem,
):
    _, outcome_count, rows, columns = tensor_hbm.shape
    pieces = 2
    width = columns // pieces
    small = [
        pltpu.make_async_copy(selected_hbm, selected_ref, small_sem.at[0]),
        pltpu.make_async_copy(vectors_hbm, vectors_ref, small_sem.at[1]),
        pltpu.make_async_copy(fresh_hbm, sent_ref.at[pl.ds(columns // (2 * rows), fresh_hbm.shape[0])], small_sem.at[2]),
    ]
    large = []
    for piece in range(pieces):
        columns_of = pl.ds(piece * width, width)
        large.append(
            pltpu.make_async_copy(
                tensor_hbm.at[0, :, :, columns_of],
                tensor_ref.at[:, :, columns_of],
                tensor_sem.at[piece],
            )
        )
    for copy in small + large:
        copy.start()
    for copy in small:
        copy.wait()
    left = left_operand(vectors_ref[0], selected_ref[0, 0:1], outcome_count)
    for piece in range(pieces):
        large[piece].wait()
        span = slice(piece * width, (piece + 1) * width)
        upper, rest = halves(tensor_ref[:, :, span].reshape(outcome_count * rows, width))
        first = piece * width // (2 * rows)
        place_product(left, upper, rest, first, rows, lax.axis_index("core"), kept_ref, sent_ref)


def split_kernel(tensor_ref, own_ref, other_ref):
    _, rows, columns = tensor_ref.shape
    own_first = lax.axis_index("core") == 0
    lane = lax.broadcasted_iota(jnp.int32, (rows, 128), 1)
    stacked = tensor_ref.shape[0] * rows
    for outcome in range(tensor_ref.shape[0]):
        band = slice(outcome * rows, (outcome + 1) * rows)
        low_band = slice(stacked + outcome * rows, stacked + (outcome + 1) * rows)
        for group in range(columns // 768):
            tile = [tensor_ref[outcome, :, group * 768 + 128 * i : group * 768 + 128 * (i + 1)] for i in range(6)]
            t0 = pltpu.roll(tile[0], 32, 1)
            t1 = pltpu.roll(tile[1], 32, 1)
            t2, t2b = pltpu.roll(tile[2], 32, 1), pltpu.roll(tile[2], 64, 1)
            t3, t3b = pltpu.roll(tile[3], 64, 1), pltpu.roll(tile[3], 96, 1)
            t4 = pltpu.roll(tile[4], 96, 1)
            t5 = pltpu.roll(tile[5], 96, 1)
            even = [
                jnp.where(lane < 96, tile[0], t1),
                jnp.where(lane < 32, t1, jnp.where(lane < 64, t2, t3)),
                jnp.where(lane < 32, t3, jnp.where(lane < 96, t4, t5)),
            ]
            odd = [
                jnp.where(lane < 32, t0, jnp.where(lane < 96, t1, t2b)),
                jnp.where(lane < 64, t2b, jnp.where(lane < 96, t3b, t4)),
                jnp.where(lane < 32, t4, tile[5]),
            ]
            for i in range(3):
                span = slice(group * 384 + 128 * i, group * 384 + 128 * (i + 1))
                upper, rest = halves(jnp.where(own_first, even[i], odd[i]))
                own_ref[band, span] = upper
                own_ref[low_band, span] = rest
                other_ref[band, span] = jnp.where(own_first, odd[i], even[i])


def later_kernel(
    tick, selected_ref, fresh_ref, received_ref, straight_ref, crossed_ref, own_ref, other_ref, paired_ref
):
    stacked, columns = other_ref.shape
    rows = straight_ref.shape[0]
    chips = columns // rows
    first = lax.axis_index("site") == 0
    selected = selected_ref[0, tick : tick + 1]
    mine = jnp.where(first, fresh_ref[tick - 1], straight_ref[...])
    theirs = jnp.where(first, received_ref[chips + tick - 1], crossed_ref[...])
    left = [left_operand(vectors, selected, stacked // rows) for vectors in (mine, theirs)]
    left = jnp.concatenate(left, axis=1)
    pieces = 2
    width = columns // pieces
    for piece in range(pieces):
        span = slice(piece * width, (piece + 1) * width)
        upper, rest = own_ref[:stacked, span], own_ref[stacked:, span]
        other_upper, other_rest = halves(other_ref[:, span])
        right = [upper, rest, upper, other_upper, other_rest, other_upper]
        product = jnp.dot(left, jnp.concatenate(right, axis=0), preferred_element_type=jnp.float32)
        blocks = product.T.reshape(chips // pieces, rows, product.shape[0])
        paired_ref[piece * chips // pieces : (piece + 1) * chips // pieces] = blocks


def cost(stacked, columns, samples, read):
    return pl.CostEstimate(
        flops=6 * stacked * columns * samples, bytes_accessed=read, transcendentals=0
    )


def first_product(outcomes, panels, fresh, site_tensor):
    _, outcome_count, rows, columns = site_tensor.shape
    samples = panels.shape[-1]
    stacked = outcome_count * rows
    chips = columns // (2 * rows)
    in_hbm = [
        pltpu.with_memory_space_constraint(a, pltpu.HBM)
        for a in (outcomes, panels, fresh, site_tensor)
    ]
    return pl.pallas_call(
        first_kernel,
        out_shape=[
            pltpu.VMEM((chips, rows, samples), jnp.float32),
            pltpu.VMEM((chips + fresh.shape[0], rows, samples), jnp.float32),
            pltpu.VMEM((outcome_count, rows, columns), jnp.float32),
            pltpu.VMEM(outcomes.shape, outcomes.dtype),
        ],
        in_specs=[HBM] * 4,
        out_specs=[VMEM] * 4,
        scratch_shapes=[
            pltpu.VMEM(panels.shape, panels.dtype),
            pltpu.SemaphoreType.DMA((3,)),
            pltpu.SemaphoreType.DMA((2,)),
        ],
        compiler_params=PARAMS,
        cost_estimate=cost(stacked, columns, samples, 4 * stacked * columns),
        name="first_product",
    )(*in_hbm)


def split_columns(tensor):
    outcome_count, rows, columns = tensor.shape
    stacked = outcome_count * rows
    return pl.pallas_call(
        split_kernel,
        out_shape=[
            pltpu.VMEM((2 * stacked, columns // 2), jnp.bfloat16),
            pltpu.VMEM((stacked, columns // 2), jnp.float32),
        ],
        in_specs=[VMEM],
        out_specs=[VMEM] * 2,
        compiler_params=PARAMS,
        cost_estimate=cost(stacked, columns, 128, 0),
        name="split_columns",
    )(tensor)


def later_product(tick, selected, fresh, received, straight, crossed, own, other):
    rows, samples = straight.shape
    stacked, columns = other.shape
    return pl.pallas_call(
        functools.partial(later_kernel, tick),
        out_shape=pltpu.VMEM((columns // rows, rows, samples), jnp.float32),
        in_specs=[VMEM] * 7,
        out_specs=VMEM,
        compiler_params=PARAMS,
        cost_estimate=cost(2 * stacked, columns, samples, 4 * columns * samples),
        name="later_product",
    )(selected, fresh, received, straight, crossed, own, other)


def pair_kernel(kept_ref, received_ref, paired_ref):
    paired_ref[...] = kept_ref[...] + received_ref[: kept_ref.shape[0]]


def pair_sum(kept, received):
    return pl.pallas_call(
        pair_kernel,
        out_shape=pltpu.VMEM(kept.shape, kept.dtype),
        in_specs=[VMEM] * 2,
        out_specs=VMEM,
        compiler_params=pltpu.CompilerParams(vmem_limit_bytes=4 * 1024 * 1024),
        cost_estimate=pl.CostEstimate(flops=10**11, bytes_accessed=10**8, transcendentals=0),
        name="pair_sum",
    )(kept, received)


def swapped(value):
    return lax.ppermute(value, "core", [(0, 1), (1, 0)])


def chip_sum(paired):
    arrived = lax.all_to_all(paired, CHIPS, 0, 0, tiled=True)
    total = functools.reduce(jnp.add, [arrived[chip] for chip in range(arrived.shape[0])])
    return lax.optimization_barrier(total)


def on_device(site_tensor, panels, fresh, outcomes):
    steps = [(i, i + 1) for i in range(lax.axis_size("site") - 1)]
    straight_pairs = [(2 * i + core, 2 * j + core) for i, j in steps for core in range(2)]
    crossed_pairs = [(2 * i + core, 2 * j + 1 - core) for i, j in steps for core in range(2)]
    kept, sent, tensor, selected = first_product(outcomes, panels, fresh, site_tensor)
    received = swapped(sent)
    own, other = split_columns(tensor)
    other = swapped(other)
    results = [chip_sum(pair_sum(kept, received))]
    for tick in range(1, TICKS):
        straight = lax.ppermute(results[-1], ("site", "core"), straight_pairs)
        crossed = lax.ppermute(results[-1], ("site", "core"), crossed_pairs)
        results.append(
            chip_sum(later_product(tick, selected, fresh, received, straight, crossed, own, other))
        )
    return jnp.stack(results, 0)[None]


def solution(mesh):
    sites, bonds = mesh.devices.shape
    side = round((bonds // 2) ** 0.5)
    split = Mesh(mesh.devices.reshape(sites, side, side, 2), ("site", "y", "x", "core"))
    placed = (
        P("site", None, BOND, None),
        P("site", BOND, None),
        P(None, BOND, None),
        P("site", None, None),
    )
    return jax.shard_map(
        on_device,
        mesh=split,
        in_specs=placed,
        out_specs=P("site", None, BOND, None),
        check_vma=False,
    )
```

```python
import functools

import jax
import jax.numpy as jnp
from jax import lax
from jax.experimental import pallas as pl
from jax.experimental.pallas import tpu as pltpu
from jax.sharding import Mesh, PartitionSpec as P

TICKS = 2
CHIPS = ("y", "x")
BOND = ("y", "x", "core")
PARAMS = pltpu.CompilerParams(vmem_limit_bytes=24 * 1024 * 1024)
VMEM = pl.BlockSpec(memory_space=pltpu.VMEM)
HBM = pl.BlockSpec(memory_space=pltpu.HBM)


def halves(value):
    upper = value.astype(jnp.bfloat16)
    return upper, (value - upper.astype(jnp.float32)).astype(jnp.bfloat16)


def left_operand(vectors, selected, outcome_count):
    masked = [jnp.where(selected == outcome, vectors, 0.0) for outcome in range(outcome_count)]
    upper, rest = halves(jnp.concatenate(masked, axis=0).T)
    return jnp.concatenate([upper, upper, rest], axis=1)


def place_product(left, upper, rest, first, rows, core, kept_ref, sent_ref):
    right = jnp.concatenate([upper, rest, upper], axis=0)
    product = jnp.dot(left, right, preferred_element_type=jnp.float32)
    chips = product.shape[1] // (2 * rows)
    blocks = product.T.reshape(chips, 2, rows, product.shape[0])
    kept_ref[first : first + chips] = jnp.where(core == 0, blocks[:, 0], blocks[:, 1])
    sent_ref[first : first + chips] = jnp.where(core == 0, blocks[:, 1], blocks[:, 0])


def alternate(tensor_ref, outcome, group, parity):
    at = group * 768
    tile = [tensor_ref[outcome, :, at + 128 * i : at + 128 * (i + 1)] for i in range(6)]
    lane = lax.broadcasted_iota(jnp.int32, tile[0].shape, 1)
    turned = (None, 32, 32, 64, 96, 96) if parity == 0 else (32, 32, 64, 96, 96, None)
    t = [value if by is None else pltpu.roll(value, by, 1) for value, by in zip(tile, turned)]
    if parity == 0:
        return [
            jnp.where(lane < 96, t[0], t[1]),
            jnp.where(lane < 32, t[1], jnp.where(lane < 64, t[2], t[3])),
            jnp.where(lane < 32, t[3], jnp.where(lane < 96, t[4], t[5])),
        ]
    return [
        jnp.where(lane < 32, t[0], jnp.where(lane < 96, t[1], t[2])),
        jnp.where(lane < 64, t[2], jnp.where(lane < 96, t[3], t[4])),
        jnp.where(lane < 32, t[4], t[5]),
    ]


def first_kernel(
    selected_hbm, vectors_hbm, fresh_hbm, tensor_hbm,
    kept_ref, sent_ref, tensor_ref, other_ref, selected_ref,
    vectors_ref, small_sem, tensor_sem,
):
    _, outcome_count, rows, columns = tensor_hbm.shape
    pieces = 2
    width = columns // pieces
    small = [
        pltpu.make_async_copy(selected_hbm, selected_ref, small_sem.at[0]),
        pltpu.make_async_copy(vectors_hbm, vectors_ref, small_sem.at[1]),
        pltpu.make_async_copy(fresh_hbm, sent_ref.at[pl.ds(columns // (2 * rows), fresh_hbm.shape[0])], small_sem.at[2]),
    ]
    large = []
    for piece in range(pieces):
        columns_of = pl.ds(piece * width, width)
        large.append(
            pltpu.make_async_copy(
                tensor_hbm.at[0, :, :, columns_of],
                tensor_ref.at[:, :, columns_of],
                tensor_sem.at[piece],
            )
        )
    for copy in small + large:
        copy.start()
    for copy in small:
        copy.wait()
    left = left_operand(vectors_ref[0], selected_ref[0, 0:1], outcome_count)
    for piece in range(pieces):
        large[piece].wait()
        span = slice(piece * width, (piece + 1) * width)
        upper, rest = halves(tensor_ref[:, :, span].reshape(outcome_count * rows, width))
        first = piece * width // (2 * rows)
        place_product(left, upper, rest, first, rows, lax.axis_index("core"), kept_ref, sent_ref)
        for parity in range(2):

            @pl.when(lax.axis_index("core") == 1 - parity)
            def _():
                for outcome in range(outcome_count):
                    for group in range(piece * width // 768, (piece + 1) * width // 768):
                        for i, tile in enumerate(alternate(tensor_ref, outcome, group, parity)):
                            begin = group * 384 + 128 * i
                            other_ref[outcome * rows : (outcome + 1) * rows, begin : begin + 128] = tile


def own_kernel(tensor_ref, own_ref):
    _, rows, columns = tensor_ref.shape
    stacked = tensor_ref.shape[0] * rows
    core = lax.axis_index("core")
    for parity in range(2):

        @pl.when(core == parity)
        def _():
            for outcome in range(tensor_ref.shape[0]):
                for group in range(columns // 768):
                    for i, tile in enumerate(alternate(tensor_ref, outcome, group, parity)):
                        span = slice(group * 384 + 128 * i, group * 384 + 128 * (i + 1))
                        first = outcome * rows
                        upper, rest = halves(tile)
                        own_ref[first : first + rows, span] = upper
                        own_ref[stacked + first : stacked + first + rows, span] = rest


def later_kernel(
    tick, selected_ref, fresh_ref, received_ref, straight_ref, crossed_ref, own_ref, other_ref, paired_ref
):
    stacked, columns = other_ref.shape
    rows = straight_ref.shape[0]
    chips = columns // rows
    first = lax.axis_index("site") == 0
    selected = selected_ref[0, tick : tick + 1]
    mine = jnp.where(first, fresh_ref[tick - 1], straight_ref[...])
    theirs = jnp.where(first, received_ref[chips + tick - 1], crossed_ref[...])
    left = [left_operand(vectors, selected, stacked // rows) for vectors in (mine, theirs)]
    left = jnp.concatenate(left, axis=1)
    pieces = 2
    width = columns // pieces
    for piece in range(pieces):
        span = slice(piece * width, (piece + 1) * width)
        upper, rest = own_ref[:stacked, span], own_ref[stacked:, span]
        other_upper, other_rest = halves(other_ref[:, span])
        right = [upper, rest, upper, other_upper, other_rest, other_upper]
        product = jnp.dot(left, jnp.concatenate(right, axis=0), preferred_element_type=jnp.float32)
        blocks = product.T.reshape(chips // pieces, rows, product.shape[0])
        paired_ref[piece * chips // pieces : (piece + 1) * chips // pieces] = blocks


def cost(stacked, columns, samples, read):
    return pl.CostEstimate(
        flops=6 * stacked * columns * samples, bytes_accessed=read, transcendentals=0
    )


def first_product(outcomes, panels, fresh, site_tensor):
    _, outcome_count, rows, columns = site_tensor.shape
    samples = panels.shape[-1]
    stacked = outcome_count * rows
    chips = columns // (2 * rows)
    in_hbm = [
        pltpu.with_memory_space_constraint(a, pltpu.HBM)
        for a in (outcomes, panels, fresh, site_tensor)
    ]
    return pl.pallas_call(
        first_kernel,
        out_shape=[
            pltpu.VMEM((chips, rows, samples), jnp.float32),
            pltpu.VMEM((chips + fresh.shape[0], rows, samples), jnp.float32),
            pltpu.VMEM((outcome_count, rows, columns), jnp.float32),
            pltpu.VMEM((stacked, columns // 2), jnp.float32),
            pltpu.VMEM(outcomes.shape, outcomes.dtype),
        ],
        in_specs=[HBM] * 4,
        out_specs=[VMEM] * 5,
        scratch_shapes=[
            pltpu.VMEM(panels.shape, panels.dtype),
            pltpu.SemaphoreType.DMA((3,)),
            pltpu.SemaphoreType.DMA((2,)),
        ],
        compiler_params=PARAMS,
        cost_estimate=cost(stacked, columns, samples, 4 * stacked * columns),
        name="first_product",
    )(*in_hbm)


def own_columns(tensor):
    outcome_count, rows, columns = tensor.shape
    stacked = outcome_count * rows
    return pl.pallas_call(
        own_kernel,
        out_shape=pltpu.VMEM((2 * stacked, columns // 2), jnp.bfloat16),
        in_specs=[VMEM],
        out_specs=VMEM,
        compiler_params=PARAMS,
        cost_estimate=cost(stacked, columns, 256, 0),
        name="own_columns",
    )(tensor)


def later_product(tick, selected, fresh, received, straight, crossed, own, other):
    rows, samples = straight.shape
    stacked, columns = other.shape
    return pl.pallas_call(
        functools.partial(later_kernel, tick),
        out_shape=pltpu.VMEM((columns // rows, rows, samples), jnp.float32),
        in_specs=[VMEM] * 7,
        out_specs=VMEM,
        compiler_params=PARAMS,
        cost_estimate=cost(2 * stacked, columns, samples, 4 * columns * samples),
        name="later_product",
    )(selected, fresh, received, straight, crossed, own, other)


def pair_kernel(kept_ref, received_ref, paired_ref):
    paired_ref[...] = kept_ref[...] + received_ref[: kept_ref.shape[0]]


def pair_sum(kept, received):
    return pl.pallas_call(
        pair_kernel,
        out_shape=pltpu.VMEM(kept.shape, kept.dtype),
        in_specs=[VMEM] * 2,
        out_specs=VMEM,
        compiler_params=pltpu.CompilerParams(vmem_limit_bytes=4 * 1024 * 1024),
        cost_estimate=pl.CostEstimate(flops=10**11, bytes_accessed=10**8, transcendentals=0),
        name="pair_sum",
    )(kept, received)


def swapped(value):
    return lax.ppermute(value, "core", [(0, 1), (1, 0)])


def chip_sum(paired):
    arrived = lax.all_to_all(paired, CHIPS, 0, 0, tiled=True)
    total = functools.reduce(jnp.add, [arrived[chip] for chip in range(arrived.shape[0])])
    return lax.optimization_barrier(total)


def on_device(site_tensor, panels, fresh, outcomes):
    steps = [(i, i + 1) for i in range(lax.axis_size("site") - 1)]
    straight_pairs = [(2 * i + core, 2 * j + core) for i, j in steps for core in range(2)]
    crossed_pairs = [(2 * i + core, 2 * j + 1 - core) for i, j in steps for core in range(2)]
    kept, sent, tensor, other, selected = first_product(outcomes, panels, fresh, site_tensor)
    received = swapped(sent)
    other = swapped(other)
    results = [chip_sum(pair_sum(kept, received))]
    for tick in range(1, TICKS):
        straight = lax.ppermute(results[-1], ("site", "core"), straight_pairs)
        crossed = lax.ppermute(results[-1], ("site", "core"), crossed_pairs)
        own = own_columns(tensor)
        results.append(
            chip_sum(later_product(tick, selected, fresh, received, straight, crossed, own, other))
        )
    return jnp.stack(results, 0)[None]


def solution(mesh):
    sites, bonds = mesh.devices.shape
    side = round((bonds // 2) ** 0.5)
    split = Mesh(mesh.devices.reshape(sites, side, side, 2), ("site", "y", "x", "core"))
    placed = (
        P("site", None, BOND, None),
        P("site", BOND, None),
        P(None, BOND, None),
        P("site", None, None),
    )
    return jax.shard_map(
        on_device,
        mesh=split,
        in_specs=placed,
        out_specs=P("site", None, BOND, None),
        check_vma=False,
    )
```

```python
import functools

import jax
import jax.numpy as jnp
from jax import lax
from jax.experimental import pallas as pl
from jax.experimental.pallas import tpu as pltpu
from jax.sharding import Mesh, PartitionSpec as P

TICKS = 2
CHIPS = ("y", "x")
BOND = ("y", "x", "core")
PARAMS = pltpu.CompilerParams(vmem_limit_bytes=24 * 1024 * 1024)
VMEM = pl.BlockSpec(memory_space=pltpu.VMEM)
HBM = pl.BlockSpec(memory_space=pltpu.HBM)


def halves(value):
    upper = value.astype(jnp.bfloat16)
    return upper, (value - upper.astype(jnp.float32)).astype(jnp.bfloat16)


def left_operand(vectors, selected, outcome_count):
    masked = [jnp.where(selected == outcome, vectors, 0.0) for outcome in range(outcome_count)]
    upper, rest = halves(jnp.concatenate(masked, axis=0).T)
    return jnp.concatenate([upper, upper, rest], axis=1)


def place_product(left, upper, rest, first, rows, core, kept_ref, sent_ref):
    right = jnp.concatenate([upper, rest, upper], axis=0)
    product = jnp.dot(left, right, preferred_element_type=jnp.float32)
    chips = product.shape[1] // (2 * rows)
    blocks = product.T.reshape(chips, 2, rows, product.shape[0])
    kept_ref[first : first + chips] = jnp.where(core == 0, blocks[:, 0], blocks[:, 1])
    sent_ref[first : first + chips] = jnp.where(core == 0, blocks[:, 1], blocks[:, 0])


def first_kernel(
    selected_hbm, vectors_hbm, tensor_hbm,
    kept_ref, sent_ref, tensor_ref, selected_ref,
    vectors_ref, small_sem, tensor_sem,
):
    _, outcome_count, rows, columns = tensor_hbm.shape
    pieces = 2
    width = columns // pieces
    small = [
        pltpu.make_async_copy(selected_hbm, selected_ref, small_sem.at[0]),
        pltpu.make_async_copy(vectors_hbm, vectors_ref, small_sem.at[1]),
    ]
    large = []
    for piece in range(pieces):
        columns_of = pl.ds(piece * width, width)
        large.append(
            pltpu.make_async_copy(
                tensor_hbm.at[0, :, :, columns_of],
                tensor_ref.at[:, :, columns_of],
                tensor_sem.at[piece],
            )
        )
    for copy in small + large:
        copy.start()
    for copy in small:
        copy.wait()
    left = left_operand(vectors_ref[0], selected_ref[0, 0:1], outcome_count)
    for piece in range(pieces):
        large[piece].wait()
        span = slice(piece * width, (piece + 1) * width)
        upper, rest = halves(tensor_ref[:, :, span].reshape(outcome_count * rows, width))
        first = piece * width // (2 * rows)
        place_product(left, upper, rest, first, rows, lax.axis_index("core"), kept_ref, sent_ref)


def halves_kernel(tensor_ref, halves_ref):
    outcome_count, rows, _ = tensor_ref.shape
    stacked = outcome_count * rows
    for outcome in range(outcome_count):
        first = outcome * rows
        upper, rest = halves(tensor_ref[outcome])
        halves_ref[first : first + rows] = upper
        halves_ref[stacked + first : stacked + first + rows] = rest


def later_kernel(tick, selected_ref, fresh_ref, passed_ref, halves_ref, kept_ref, sent_ref):
    rows = passed_ref.shape[0]
    vectors = jnp.where(lax.axis_index("site") == 0, fresh_ref[tick - 1], passed_ref[...])
    stacked, columns = halves_ref.shape[0] // 2, halves_ref.shape[1]
    left = left_operand(vectors, selected_ref[0, tick : tick + 1], stacked // rows)
    pieces = 2
    width = columns // pieces
    for piece in range(pieces):
        span = slice(piece * width, (piece + 1) * width)
        first = piece * width // (2 * rows)
        upper, rest = halves_ref[:stacked, span], halves_ref[stacked:, span]
        place_product(left, upper, rest, first, rows, lax.axis_index("core"), kept_ref, sent_ref)


def cost(stacked, columns, samples, read):
    return pl.CostEstimate(
        flops=6 * stacked * columns * samples, bytes_accessed=read, transcendentals=0
    )


def first_product(outcomes, panels, site_tensor):
    _, outcome_count, rows, columns = site_tensor.shape
    samples = panels.shape[-1]
    stacked = outcome_count * rows
    block = pltpu.VMEM((columns // (2 * rows), rows, samples), jnp.float32)
    whole = pltpu.VMEM((outcome_count, rows, columns), jnp.float32)
    in_hbm = [pltpu.with_memory_space_constraint(a, pltpu.HBM) for a in (outcomes, panels, site_tensor)]
    return pl.pallas_call(
        first_kernel,
        out_shape=[block, block, whole, pltpu.VMEM(outcomes.shape, outcomes.dtype)],
        in_specs=[HBM, HBM, HBM],
        out_specs=[VMEM] * 4,
        scratch_shapes=[
            pltpu.VMEM(panels.shape, panels.dtype),
            pltpu.SemaphoreType.DMA((2,)),
            pltpu.SemaphoreType.DMA((2,)),
        ],
        compiler_params=PARAMS,
        cost_estimate=cost(stacked, columns, samples, 4 * stacked * columns),
        name="first_product",
    )(*in_hbm)


def tensor_halves(tensor):
    outcome_count, rows, columns = tensor.shape
    return pl.pallas_call(
        halves_kernel,
        out_shape=pltpu.VMEM((2 * outcome_count * rows, columns), jnp.bfloat16),
        in_specs=[VMEM],
        out_specs=VMEM,
        compiler_params=PARAMS,
        cost_estimate=cost(outcome_count * rows, columns, 128, 0),
        name="tensor_halves",
    )(tensor)


def later_product(tick, selected, fresh, passed, both):
    rows, samples = passed.shape
    stacked, columns = both.shape[0] // 2, both.shape[1]
    block = pltpu.VMEM((columns // (2 * rows), rows, samples), jnp.float32)
    return pl.pallas_call(
        functools.partial(later_kernel, tick),
        out_shape=[block, block],
        in_specs=[VMEM, VMEM, VMEM, VMEM],
        out_specs=[VMEM] * 2,
        compiler_params=PARAMS,
        cost_estimate=cost(stacked, columns, samples, 4 * columns * samples),
        name="later_product",
    )(selected, fresh, passed, both)


def scatter_sum(kept, sent):
    paired = kept + lax.ppermute(sent, "core", [(0, 1), (1, 0)])
    arrived = lax.all_to_all(paired, CHIPS, 0, 0, tiled=True)
    total = functools.reduce(jnp.add, [arrived[chip] for chip in range(arrived.shape[0])])
    return lax.optimization_barrier(total)


def on_device(site_tensor, panels, fresh, outcomes):
    sites = lax.axis_size("site")
    kept, sent, tensor, selected = first_product(outcomes, panels, site_tensor)
    results = [scatter_sum(kept, sent)]
    for tick in range(1, TICKS):
        passed = lax.ppermute(results[-1], "site", [(i, i + 1) for i in range(sites - 1)])
        both = tensor_halves(tensor)
        results.append(scatter_sum(*later_product(tick, selected, fresh, passed, both)))
    return jnp.stack(results, 0)[None]


def solution(mesh):
    sites, bonds = mesh.devices.shape
    side = round((bonds // 2) ** 0.5)
    split = Mesh(mesh.devices.reshape(sites, side, side, 2), ("site", "y", "x", "core"))
    placed = (
        P("site", None, BOND, None),
        P("site", BOND, None),
        P(None, BOND, None),
        P("site", None, None),
    )
    return jax.shard_map(
        on_device,
        mesh=split,
        in_specs=placed,
        out_specs=P("site", None, BOND, None),
        check_vma=False,
    )
```

```python
import functools

import jax
import jax.numpy as jnp
from jax import lax
from jax.experimental import pallas as pl
from jax.experimental.pallas import tpu as pltpu
from jax.sharding import Mesh, PartitionSpec as P

TICKS = 2
CHIPS = ("y", "x")
BOND = ("y", "x", "core")
PARAMS = pltpu.CompilerParams(vmem_limit_bytes=24 * 1024 * 1024)
VMEM = pl.BlockSpec(memory_space=pltpu.VMEM)
HBM = pl.BlockSpec(memory_space=pltpu.HBM)


def halves(value):
    upper = value.astype(jnp.bfloat16)
    return upper, (value - upper.astype(jnp.float32)).astype(jnp.bfloat16)


def left_operand(vectors, selected, outcome_count):
    masked = [jnp.where(selected == outcome, vectors, 0.0) for outcome in range(outcome_count)]
    upper, rest = halves(jnp.concatenate(masked, axis=0).T)
    return jnp.concatenate([upper, upper, rest], axis=1)


def place_product(left, upper, rest, first, rows, core, kept_ref, sent_ref):
    right = jnp.concatenate([upper, rest, upper], axis=0)
    product = jnp.dot(left, right, preferred_element_type=jnp.float32)
    chips = product.shape[1] // (2 * rows)
    blocks = product.T.reshape(chips, 2, rows, product.shape[0])
    kept_ref[first : first + chips] = jnp.where(core == 0, blocks[:, 0], blocks[:, 1])
    sent_ref[first : first + chips] = jnp.where(core == 0, blocks[:, 1], blocks[:, 0])


def first_kernel(
    selected_hbm, vectors_hbm, tensor_hbm,
    kept_ref, sent_ref, tensor_ref, selected_ref,
    vectors_ref, small_sem, tensor_sem,
):
    _, outcome_count, rows, columns = tensor_hbm.shape
    pieces = 2
    width = columns // pieces
    small = [
        pltpu.make_async_copy(selected_hbm, selected_ref, small_sem.at[0]),
        pltpu.make_async_copy(vectors_hbm, vectors_ref, small_sem.at[1]),
    ]
    large = []
    for piece in range(pieces):
        columns_of = pl.ds(piece * width, width)
        large.append(
            pltpu.make_async_copy(
                tensor_hbm.at[0, :, :, columns_of],
                tensor_ref.at[:, :, columns_of],
                tensor_sem.at[piece],
            )
        )
    for copy in small + large:
        copy.start()
    for copy in small:
        copy.wait()
    left = left_operand(vectors_ref[0], selected_ref[0, 0:1], outcome_count)
    for piece in range(pieces):
        large[piece].wait()
        span = slice(piece * width, (piece + 1) * width)
        upper, rest = halves(tensor_ref[:, :, span].reshape(outcome_count * rows, width))
        first = piece * width // (2 * rows)
        place_product(left, upper, rest, first, rows, lax.axis_index("core"), kept_ref, sent_ref)


def halves_kernel(tensor_ref, halves_ref):
    outcome_count, rows, _ = tensor_ref.shape
    stacked = outcome_count * rows
    for outcome in range(outcome_count):
        first = outcome * rows
        upper, rest = halves(tensor_ref[outcome])
        halves_ref[first : first + rows] = upper
        halves_ref[stacked + first : stacked + first + rows] = rest


def later_kernel(tick, selected_ref, fresh_ref, passed_ref, halves_ref, kept_ref, sent_ref):
    rows = passed_ref.shape[0]
    vectors = jnp.where(lax.axis_index("site") == 0, fresh_ref[tick - 1], passed_ref[...])
    stacked, columns = halves_ref.shape[0] // 2, halves_ref.shape[1]
    left = left_operand(vectors, selected_ref[0, tick : tick + 1], stacked // rows)
    pieces = 2
    width = columns // pieces
    for piece in range(pieces):
        span = slice(piece * width, (piece + 1) * width)
        first = piece * width // (2 * rows)
        upper, rest = halves_ref[:stacked, span], halves_ref[stacked:, span]
        place_product(left, upper, rest, first, rows, lax.axis_index("core"), kept_ref, sent_ref)


def cost(stacked, columns, samples, read):
    return pl.CostEstimate(
        flops=6 * stacked * columns * samples, bytes_accessed=read, transcendentals=0
    )


def first_product(outcomes, panels, site_tensor):
    _, outcome_count, rows, columns = site_tensor.shape
    samples = panels.shape[-1]
    stacked = outcome_count * rows
    block = pltpu.VMEM((columns // (2 * rows), rows, samples), jnp.float32)
    whole = pltpu.VMEM((outcome_count, rows, columns), jnp.float32)
    in_hbm = [pltpu.with_memory_space_constraint(a, pltpu.HBM) for a in (outcomes, panels, site_tensor)]
    return pl.pallas_call(
        first_kernel,
        out_shape=[block, block, whole, pltpu.VMEM(outcomes.shape, outcomes.dtype)],
        in_specs=[HBM, HBM, HBM],
        out_specs=[VMEM] * 4,
        scratch_shapes=[
            pltpu.VMEM(panels.shape, panels.dtype),
            pltpu.SemaphoreType.DMA((2,)),
            pltpu.SemaphoreType.DMA((2,)),
        ],
        compiler_params=PARAMS,
        cost_estimate=cost(stacked, columns, samples, 4 * stacked * columns),
        name="first_product",
    )(*in_hbm)


def tensor_halves(tensor):
    outcome_count, rows, columns = tensor.shape
    return pl.pallas_call(
        halves_kernel,
        out_shape=pltpu.VMEM((2 * outcome_count * rows, columns), jnp.bfloat16),
        in_specs=[VMEM],
        out_specs=VMEM,
        compiler_params=PARAMS,
        cost_estimate=cost(outcome_count * rows, columns, 128, 0),
        name="tensor_halves",
    )(tensor)


def later_product(tick, selected, fresh, passed, both):
    rows, samples = passed.shape
    stacked, columns = both.shape[0] // 2, both.shape[1]
    block = pltpu.VMEM((columns // (2 * rows), rows, samples), jnp.float32)
    return pl.pallas_call(
        functools.partial(later_kernel, tick),
        out_shape=[block, block],
        in_specs=[VMEM, VMEM, VMEM, VMEM],
        out_specs=[VMEM] * 2,
        compiler_params=PARAMS,
        cost_estimate=cost(stacked, columns, samples, 4 * columns * samples),
        name="later_product",
    )(selected, fresh, passed, both)


def last_kernel(earlier_ref, arrived_ref, out_hbm, total_ref, sem):
    first = pltpu.make_async_copy(earlier_ref, out_hbm.at[0, 0], sem.at[0])
    first.start()
    total = arrived_ref[0]
    for chip in range(1, arrived_ref.shape[0]):
        total = total + arrived_ref[chip]
    total_ref[...] = total
    second = pltpu.make_async_copy(total_ref, out_hbm.at[0, 1], sem.at[1])
    second.start()
    first.wait()
    second.wait()


def last_sum(earlier, arrived):
    rows, samples = earlier.shape
    return pl.pallas_call(
        last_kernel,
        out_shape=jax.ShapeDtypeStruct((1, TICKS, rows, samples), earlier.dtype),
        in_specs=[VMEM] * 2,
        out_specs=HBM,
        scratch_shapes=[pltpu.VMEM(earlier.shape, earlier.dtype), pltpu.SemaphoreType.DMA((2,))],
        compiler_params=pltpu.CompilerParams(vmem_limit_bytes=4 * 1024 * 1024),
        name="last_sum",
    )(earlier, arrived)


def scatter(kept, sent):
    paired = kept + lax.ppermute(sent, "core", [(0, 1), (1, 0)])
    return lax.all_to_all(paired, CHIPS, 0, 0, tiled=True)


def on_device(site_tensor, panels, fresh, outcomes):
    sites = lax.axis_size("site")
    kept, sent, tensor, selected = first_product(outcomes, panels, site_tensor)
    arrived = scatter(kept, sent)
    earlier = functools.reduce(jnp.add, [arrived[chip] for chip in range(arrived.shape[0])])
    passed = lax.ppermute(earlier, "site", [(i, i + 1) for i in range(sites - 1)])
    both = tensor_halves(tensor)
    return last_sum(earlier, scatter(*later_product(1, selected, fresh, passed, both)))


def solution(mesh):
    sites, bonds = mesh.devices.shape
    side = round((bonds // 2) ** 0.5)
    split = Mesh(mesh.devices.reshape(sites, side, side, 2), ("site", "y", "x", "core"))
    placed = (
        P("site", None, BOND, None),
        P("site", BOND, None),
        P(None, BOND, None),
        P("site", None, None),
    )
    return jax.shard_map(
        on_device,
        mesh=split,
        in_specs=placed,
        out_specs=P("site", None, BOND, None),
        check_vma=False,
    )
```
